256 devices in a mesh: gx: 32 (over z, y_lo, core), gy: 8 (over y_hi, x).
Axes of the slice: x: 4, y: 4 (y_hi: 2, y_lo: 2; y = y_hi * 2 + y_lo), z: 8, core: 2. Of those that a mesh axis runs over, the one named last changes fastest.
Arguments:
- image_tile: bfloat16 [256, 2048, 128], P('gy', 'gx'), may hold values from -6 to 6
- cotangent: bfloat16 [256, 2048, 128], P('gy', 'gx'), may hold values from -6 to 6
- weights: bfloat16 [3, 3, 3, 128, 128], replicated, may hold values from -0.1875 to 0.1875
Outputs:
- features: bfloat16 [256, 2048, 128], P('gy', 'gx')
- image_grad: bfloat16 [256, 2048, 128], P('gy', 'gx')
- weight_grad: float32 [3, 3, 3, 128, 128], replicated
The draws below stay inside these ranges and needn't reach their ends.
All inputs are finite; a program needn't handle non-finite values.
Results may differ from the reference program's by a relative error of at most 0.008.
Values may be sent and summed in bfloat16 or wider, within the bound.
A program may use at most 128 MiB of HBM per device.

```python
import math
import jax
import jax.numpy as jnp
from jax import lax

CH = 128
LAYERS = 3
BASE_DILATION = 32
NX = 2048
NY = 256


def level_of(key, shape, split, smallest, high):
    factor_of, own = 1.0, jax.random.fold_in(key, 6)
    for dim, parts in split:
        steps = jnp.exp(jax.random.uniform(jax.random.fold_in(own, dim), (parts,), jnp.float32, smallest / len(split), high / len(split)))
        factor_of = factor_of * jnp.repeat(steps, shape[dim] // parts).reshape([-1 if axis == dim else 1 for axis in range(len(shape))])
    return factor_of


def scatter_about(key, dims, deviation, limit, split=(), dtype=jnp.bfloat16):
    level = level_of(key, dims, split, -0.22, 0.18) if split else 1.0
    entries = jax.random.normal(key, dims, jnp.float32) * deviation * level
    return jnp.minimum(jnp.maximum(entries, -limit), limit).astype(dtype)


def setup_inputs(seed: int = 0) -> dict:
    key_list = jax.random.split(jax.random.key(seed), 4)
    return {
        "image_tile": scatter_about(key_list[0], (NY, NX, CH), 1.0, 6.0, ((0, 8), (1, 32))),
        "cotangent": scatter_about(key_list[1], (NY, NX, CH), 1.0, 6.0, ((0, 8), (1, 32))),
        "weights": scatter_about(key_list[2], (LAYERS, 3, 3, CH, CH), (9 * CH) ** -0.5, 0.1875),
    }


def tap_rows(padded, i, dilation, row_count, col_count, channels):
    pieces = [padded[i * dilation:i * dilation + row_count, j * dilation:j * dilation + col_count] for j in range(3)]
    return jnp.concatenate(pieces, axis=-1).reshape(row_count * col_count, 3 * channels)

def conv_taps(source, kernel, dilation):
    row_count, col_count, channels = source.shape
    padded = jnp.pad(source, ((dilation, dilation), (dilation, dilation), (0, 0)))
    summed = jnp.zeros((row_count * col_count, channels), jnp.float32)
    for i in range(3):
        columns = tap_rows(padded, i, dilation, row_count, col_count, channels)
        summed = summed + jnp.dot(columns, kernel[i].reshape(3 * channels, channels), preferred_element_type=jnp.float32)
    return summed.reshape(row_count, col_count, channels)

def tap_grad(source, rounded, dilation):
    row_count, col_count, channels = source.shape
    padded = jnp.pad(source, ((dilation, dilation), (dilation, dilation), (0, 0)))
    flat_grad = rounded.reshape(row_count * col_count, channels)
    results = []
    for i in range(3):
        columns = tap_rows(padded, i, dilation, row_count, col_count, channels)
        product = lax.dot_general(columns, flat_grad, (((0,), (0,)), ((), ())), preferred_element_type=jnp.float32)
        results.append(product.reshape(3, channels, channels))
    return jnp.stack(results)

def reference(image_tile, cotangent, weights):
    dilation_rates = [BASE_DILATION, 2 * BASE_DILATION, 4 * BASE_DILATION]
    scale_factor = 1.0 / math.sqrt(NY * NX)
    hidden = image_tile
    hidden_list = []
    active_list = []
    for k in range(LAYERS):
        activated = jax.nn.elu(hidden.astype(jnp.float32)).astype(jnp.bfloat16)
        mixed = conv_taps(activated, weights[k], dilation_rates[k])
        hidden_list.append(hidden)
        active_list.append(activated)
        hidden = (hidden.astype(jnp.float32) + mixed).astype(jnp.bfloat16)
    features = hidden
    upstream = cotangent.astype(jnp.float32)
    grad_list = [None, None, None]
    for k in reversed(range(LAYERS)):
        rounded = upstream.astype(jnp.bfloat16)
        grad_list[k] = tap_grad(active_list[k], rounded, dilation_rates[k])
        flipped = jnp.transpose(jnp.flip(weights[k], (0, 1)), (0, 1, 3, 2))
        back_term = conv_taps(rounded, flipped, dilation_rates[k])
        upstream = upstream + back_term * jnp.exp(jnp.minimum(hidden_list[k].astype(jnp.float32), 0.0))
    image_grad = upstream.astype(jnp.bfloat16)
    weight_grad = jnp.stack(grad_list) * scale_factor
    return (features, image_grad, weight_grad)
```

```python
import functools
import math

import jax
import jax.numpy as jnp
from jax import lax
from jax.experimental import pallas as pl
from jax.experimental.pallas import tpu as pltpu
from jax.sharding import PartitionSpec as P

SUB = 4
HALO = 224
STEPS = (1, 2, 4)
SLICE = 48


def pairs_of(step):
    return [(o, o + step) for o in range(8) if (o // step) % 2 == 0]


def wait_bytes(ref, sem):
    pltpu.make_async_copy(ref, ref, sem).wait()


def elu(h):
    v = h.astype(jnp.float32)
    return jnp.where(v > 0, v, jnp.exp(jnp.minimum(v, 0.0)) - 1.0).astype(jnp.bfloat16)


def kernel(
    rows, cols, planes, scale,
    image, cotangent, weights,
    feat_out, grad_out, wg_out,
    wv, ft, cf, cb,
    h0, a0, h1, a1, h2, a2, ct,
    u2, r1, u1, r0, feat, grad,
    wacc, rsb, rsr, zr, ags,
    w_sem, in_send, in_recv, z_send, z_recv, out_send, out_recv,
    rs_send, rs_recv, zz_send, zz_recv, ag_send, ag_recv,
):
    gx, gy = lax.axis_index("gx"), lax.axis_index("gy")
    z, c = gx // SUB, gx % SUB
    me = gy * SUB + c
    group = rows
    width = SUB * cols
    own = pl.ds(HALO, width)
    total = width + 2 * HALO

    def at(q):
        return {"gx": z * SUB + q % SUB, "gy": q // SUB}

    def at_plane(p):
        return {"gx": p * SUB + c, "gy": gy}

    w_copy = pltpu.make_async_copy(weights, wv, w_sem)
    w_copy.start()

    barrier = pltpu.get_barrier_semaphore()

    def greet(t, carry):
        pl.semaphore_signal(barrier, inc=1, device_id=at((me + t) % group), device_id_type=pl.DeviceIdType.MESH)
        return carry

    lax.fori_loop(1, group, greet, 0)

    def greet_plane(t, carry):
        pl.semaphore_signal(barrier, inc=1, device_id=at_plane((z + t) % planes), device_id_type=pl.DeviceIdType.MESH)
        return carry

    lax.fori_loop(1, planes, greet_plane, 0)
    pl.semaphore_wait(barrier, group - 1 + planes - 1)

    def send_in(source, ext, n):
        place = ext.at[gy, pl.ds(pl.multiple_of(HALO + c * cols, 32), cols)]

        def one(t, carry):
            q = (me + t) % group
            pltpu.make_async_remote_copy(
                src_ref=source.at[q], dst_ref=place, send_sem=in_send.at[n], recv_sem=in_recv.at[n],
                device_id=at(q), device_id_type=pl.DeviceIdType.MESH,
            ).start()
            return carry

        lax.fori_loop(1, group, one, 0)
        pltpu.make_async_copy(source.at[me], place, in_recv.at[n]).start()

    def send_halo(ext, n):
        @pl.when(z < planes - 1)
        def _():
            pltpu.make_async_remote_copy(
                src_ref=ext.at[:, pl.ds(width, HALO)], dst_ref=ext.at[:, pl.ds(0, HALO)],
                send_sem=z_send.at[n, 0], recv_sem=z_recv.at[n, 0],
                device_id=at_plane(z + 1), device_id_type=pl.DeviceIdType.MESH,
            ).start()

        @pl.when(z > 0)
        def _():
            pltpu.make_async_remote_copy(
                src_ref=ext.at[:, pl.ds(HALO, HALO)], dst_ref=ext.at[:, pl.ds(HALO + width, HALO)],
                send_sem=z_send.at[n, 1], recv_sem=z_recv.at[n, 1],
                device_id=at_plane(z - 1), device_id_type=pl.DeviceIdType.MESH,
            ).start()

    def wait_halo(ext, n):
        @pl.when(z > 0)
        def _():
            wait_bytes(ext.at[:, pl.ds(0, HALO)], z_recv.at[n, 0])

        @pl.when(z < planes - 1)
        def _():
            wait_bytes(ext.at[:, pl.ds(HALO + width, HALO)], z_recv.at[n, 1])

    def zero_edges(ext):
        @pl.when(z == 0)
        def _():
            ext[:, 0:HALO, :] = jnp.zeros((8, HALO, 128), ext.dtype)

        @pl.when(z == planes - 1)
        def _():
            ext[:, HALO + width :, :] = jnp.zeros((8, HALO, 128), ext.dtype)

    def send_out(block, out, n):
        def one(t, carry):
            q = (me + t) % group
            pltpu.make_async_remote_copy(
                src_ref=block.at[q // SUB, pl.ds(pl.multiple_of((q % SUB) * cols, 32), cols)], dst_ref=out.at[me],
                send_sem=out_send.at[n], recv_sem=out_recv.at[n],
                device_id=at(q), device_id_type=pl.DeviceIdType.MESH,
            ).start()
            return carry

        lax.fori_loop(1, group, one, 0)
        pltpu.make_async_copy(
            block.at[gy, pl.ds(pl.multiple_of(c * cols, 32), cols)], out.at[me], out_recv.at[n]
        ).start()

    send_in(image, h0, 0)
    zero_edges(h0)
    zero_edges(ct)

    w_copy.wait()

    def flip(n, carry):
        k, m = n // 9, n % 9
        i, j = m // 3, m % 3
        ft[k, i, j] = wv[k, 2 - i, 2 - j].astype(jnp.float32).T.astype(jnp.bfloat16)
        return carry

    lax.fori_loop(0, 27, flip, 0)
    for src, dst in ((wv, cf), (ft, cb)):
        for k in range(3):
            for j in range(3):
                base = j * 256
                dst[k, base : base + 128, 0:128] = src[k, 1, j]
                dst[k, base : base + 128, 128:256] = src[k, 0, j]
                dst[k, base + 128 : base + 256, 0:128] = src[k, 2, j]
                dst[k, base + 128 : base + 256, 128:256] = src[k, 1, j]

    wait_bytes(h0.at[:, own], in_recv.at[0])
    send_halo(h0, 0)
    send_in(cotangent, ct, 1)
    for a in range(8):
        a0[a, HALO : HALO + width, :] = elu(h0[a, HALO : HALO + width, :])
    wait_bytes(ct.at[:, own], in_recv.at[1])
    send_halo(ct, 1)
    wait_halo(h0, 0)
    for a in range(8):
        a0[a, 0:HALO, :] = elu(h0[a, 0:HALO, :])
        a0[a, HALO + width :, :] = elu(h0[a, HALO + width :, :])

    left_in = z > 0
    right_in = z < planes - 1

    def conv(src, both, single, k, lo, emit):
        step, d = STEPS[k], 32 * STEPS[k]
        chunks = [(HALO, width, None)]
        if lo < HALO:
            chunks = [(lo, HALO - lo, left_in), chunks[0], (HALO + width, HALO - lo, right_in)]
        for start, size, inside in chunks:
            def taps(which):
                parts = []
                for j in range(3):
                    at_col = start + (j - 1) * d
                    parts += [src[r, at_col : at_col + size, :] for r in which]
                return jnp.concatenate(parts, axis=1)

            for first, second in pairs_of(step):
                acc = jnp.dot(taps((first, second)), both[k], preferred_element_type=jnp.float32)
                one, two = acc[:, 0:128], acc[:, 128:256]
                if first - step >= 0:
                    one = one + jnp.dot(
                        taps((first - step,)), single[k, 0].reshape(384, 128), preferred_element_type=jnp.float32
                    )
                if second + step < 8:
                    two = two + jnp.dot(
                        taps((second + step,)), single[k, 2].reshape(384, 128), preferred_element_type=jnp.float32
                    )
                emit(first, start, size, inside, one)
                emit(second, start, size, inside, two)

    def forward(old, new, active):
        def emit(row, start, size, inside, value):
            hid = old[row, start : start + size, :].astype(jnp.float32) + value
            if inside is not None:
                hid = jnp.where(inside, hid, 0.0)
            hid = hid.astype(jnp.bfloat16)
            if active is None:
                new[row, start - HALO : start - HALO + size, :] = hid
            else:
                new[row, start : start + size, :] = hid
                active[row, start : start + size, :] = elu(hid)

        return emit

    def backward(old, hidden, new, rounded):
        def emit(row, start, size, inside, value):
            gate = jnp.exp(jnp.minimum(hidden[row, start : start + size, :].astype(jnp.float32), 0.0))
            up = old[row, start : start + size, :].astype(jnp.float32) + value * gate
            if inside is not None:
                up = jnp.where(inside, up, 0.0)
            if new is None:
                rounded[row, start - HALO : start - HALO + size, :] = up.astype(jnp.bfloat16)
            else:
                new[row, start : start + size, :] = up
                rounded[row, start : start + size, :] = up.astype(jnp.bfloat16)

        return emit

    def kernel_grad(k, active, rounded):
        step, d = STEPS[k], 32 * STEPS[k]
        runs = [(0, step, 0, 2), (step, 8 - step, 0, 3), (8 - step, 8, 1, 3)]
        wacc[...] = jnp.zeros_like(wacc)
        for q0, q1, i0, i1 in runs:
            if q1 <= q0:
                continue
            count = (q1 - q0) * width
            left = jnp.concatenate(
                [
                    active[q0:q1, HALO + (j - 1) * d : HALO + (j - 1) * d + width, :].reshape(count, 128)
                    for j in range(3)
                ],
                axis=1,
            )
            right = jnp.concatenate(
                [
                    rounded[q0 - (i - 1) * step : q1 - (i - 1) * step, HALO : HALO + width, :].reshape(count, 128)
                    for i in range(i0, i1)
                ],
                axis=1,
            )
            wacc[:, i0 * 128 : i1 * 128] += lax.dot_general(
                left, right, (((0,), (0,)), ((), ())), preferred_element_type=jnp.float32
            )
        for i in range(3):
            for j in range(3):
                rsb[k, (i * 3 + j) * 128 : (i * 3 + j + 1) * 128, :] = wacc[
                    j * 128 : (j + 1) * 128, i * 128 : (i + 1) * 128
                ].astype(jnp.bfloat16)

        def one(t, carry):
            q = (me + t) % group

            @pl.when(q < reducers)
            def _():
                pltpu.make_async_remote_copy(
                    src_ref=rsb.at[k, pl.ds(pl.multiple_of(q * SLICE, 16), SLICE)], dst_ref=rsr.at[k, me],
                    send_sem=rs_send.at[k], recv_sem=rs_recv.at[k],
                    device_id=at(q), device_id_type=pl.DeviceIdType.MESH,
                ).start()

            return carry

        lax.fori_loop(1, group, one, 0)

        @pl.when(me < reducers)
        def _():
            pltpu.make_async_copy(
                rsb.at[k, pl.ds(pl.multiple_of(me * SLICE, 16), SLICE)], rsr.at[k, me], rs_recv.at[k]
            ).start()

    reducers = 9 * 128 // SLICE

    def sum_plane(k):
        @pl.when(me < reducers)
        def _():
            wait_bytes(rsr.at[k], rs_recv.at[k])
            part = rsr[k, 0].astype(jnp.float32)
            for n in range(1, group):
                part = part + rsr[k, n].astype(jnp.float32)
            zr[k, z] = part.astype(jnp.bfloat16)

            def one(t, carry):
                pltpu.make_async_remote_copy(
                    src_ref=zr.at[k, z], dst_ref=zr.at[k, z],
                    send_sem=zz_send.at[k], recv_sem=zz_recv.at[k],
                    device_id=at_plane((z + t) % planes), device_id_type=pl.DeviceIdType.MESH,
                ).start()
                return carry

            lax.fori_loop(1, planes, one, 0)

    def sum_planes(k):
        @pl.when(me < reducers)
        def _():
            wait_bytes(zr.at[k, pl.ds(0, planes - 1)], zz_recv.at[k])
            part = zr[k, 0].astype(jnp.float32)
            for n in range(1, planes):
                part = part + zr[k, n].astype(jnp.float32)
            ags[k] = (part * scale).astype(jnp.bfloat16)
            place = wg_out.at[k, pl.ds(pl.multiple_of(me * SLICE, 16), SLICE)]

            def one(t, carry):
                pltpu.make_async_remote_copy(
                    src_ref=ags.at[k], dst_ref=place,
                    send_sem=ag_send.at[k], recv_sem=ag_recv.at[k],
                    device_id=at((me + t) % group), device_id_type=pl.DeviceIdType.MESH,
                ).start()
                return carry

            lax.fori_loop(1, group, one, 0)
            pltpu.make_async_copy(ags.at[k], place, ag_recv.at[k]).start()

    conv(a0, cf, wv, 0, 32, forward(h0, h1, a1))
    conv(a1, cf, wv, 1, 96, forward(h1, h2, a2))
    conv(a2, cf, wv, 2, HALO, forward(h2, feat, None))
    send_out(feat, feat_out, 0)
    kernel_grad(2, a2, ct)
    wait_halo(ct, 1)
    conv(ct, cb, ft, 2, 128, backward(ct, h2, u2, r1))
    kernel_grad(1, a1, r1)
    sum_plane(2)
    conv(r1, cb, ft, 1, 192, backward(u2, h1, u1, r0))
    kernel_grad(0, a0, r0)
    sum_plane(1)
    sum_planes(2)
    conv(r0, cb, ft, 0, HALO, backward(u1, h0, None, grad))
    send_out(grad, grad_out, 1)
    sum_plane(0)
    sum_planes(1)
    sum_planes(0)

    wait_bytes(image.at[pl.ds(0, group - 1)], in_send.at[0])
    wait_bytes(image.at[pl.ds(0, group - 1)], in_send.at[1])
    for n in range(2):
        @pl.when(z < planes - 1)
        def _():
            wait_bytes(h0.at[:, pl.ds(0, HALO)], z_send.at[n, 0])

        @pl.when(z > 0)
        def _():
            wait_bytes(h0.at[:, pl.ds(0, HALO)], z_send.at[n, 1])

    wait_bytes(feat_out.at[pl.ds(0, group - 1)], out_send.at[0])
    wait_bytes(feat_out, out_recv.at[0])
    for k in range(3):
        @pl.when(me < reducers)
        def _():
            wait_bytes(rsb.at[k, pl.ds(0, (reducers - 1) * SLICE)], rs_send.at[k])
            wait_bytes(zr.at[k, pl.ds(0, planes - 1)], zz_send.at[k])
            wait_bytes(rsr.at[k, pl.ds(0, group - 1)], ag_send.at[k])

        @pl.when(me >= reducers)
        def _():
            wait_bytes(rsb.at[k], rs_send.at[k])

        wait_bytes(wg_out.at[k], ag_recv.at[k])
    wait_bytes(grad_out.at[pl.ds(0, group - 1)], out_send.at[1])
    wait_bytes(grad_out, out_recv.at[1])


def solution(mesh):
    nx, ny = mesh.shape["gx"], mesh.shape["gy"]
    planes = nx // SUB

    def shards(image, cotangent, weights):
        rows, cols, ch = image.shape
        width = SUB * cols
        total = width + 2 * HALO
        scale = 1.0 / math.sqrt(rows * ny * cols * nx)
        bf, f32 = jnp.bfloat16, jnp.float32
        dma = pltpu.SemaphoreType.DMA
        ext = pltpu.VMEM((ny, total, ch), bf)
        ext32 = pltpu.VMEM((ny, total, ch), f32)
        body = functools.partial(kernel, rows, cols, planes, scale)
        features, grad, wg = pl.pallas_call(
            body,
            out_shape=(
                jax.ShapeDtypeStruct(image.shape, bf),
                jax.ShapeDtypeStruct(image.shape, bf),
                jax.ShapeDtypeStruct((3, 9 * ch, ch), bf),
            ),
            in_specs=[pl.BlockSpec(memory_space=pl.ANY)] * 3,
            out_specs=[pl.BlockSpec(memory_space=pl.ANY)] * 3,
            scratch_shapes=[
                pltpu.VMEM((3, 3, 3, ch, ch), bf),
                pltpu.VMEM((3, 3, 3, ch, ch), bf),
                pltpu.VMEM((3, 6 * ch, 2 * ch), bf),
                pltpu.VMEM((3, 6 * ch, 2 * ch), bf),
                ext, ext, ext, ext, ext, ext, ext,
                ext32, ext, ext32, ext,
                pltpu.VMEM((ny, width, ch), bf),
                pltpu.VMEM((ny, width, ch), bf),
                pltpu.VMEM((3 * ch, 3 * ch), f32),
                pltpu.VMEM((3, 9 * ch, ch), bf),
                pltpu.VMEM((3, rows, SLICE, ch), bf),
                pltpu.VMEM((3, planes, SLICE, ch), bf),
                pltpu.VMEM((3, SLICE, ch), bf),
                dma,
                dma((2,)), dma((2,)), dma((2, 2)), dma((2, 2)), dma((2,)), dma((2,)),
                dma((3,)), dma((3,)), dma((3,)), dma((3,)), dma((3,)), dma((3,)),
            ],
            compiler_params=pltpu.CompilerParams(
                collective_id=0, has_side_effects=True, vmem_limit_bytes=56 * 1024 * 1024
            ),
        )(image, cotangent, weights)
        return features, grad, wg.reshape(3, 3, 3, ch, ch).astype(f32)

    return jax.shard_map(
        shards,
        mesh=mesh,
        in_specs=(P("gy", "gx", None), P("gy", "gx", None), P()),
        out_specs=(P("gy", "gx", None), P("gy", "gx", None), P()),
        check_vma=False,
    )
```

```python
import functools
import math

import jax
import jax.numpy as jnp
from jax import lax
from jax.experimental import pallas as pl
from jax.experimental.pallas import tpu as pltpu
from jax.sharding import PartitionSpec as P

SUB = 4
HALO = 224
STEPS = (1, 2, 4)
PIECES = ((0, 128), (128, 64), (192, 32))
SLICE, SLICES = 48, 12
HALF = SLICE * SLICES


def pairs_of(step):
    return [(o, o + step) for o in range(8) if (o // step) % 2 == 0]


def wait_bytes(ref, sem):
    pltpu.make_async_copy(ref, ref, sem).wait()


def elu(h):
    v = h.astype(jnp.float32)
    return jnp.where(v > 0, v, jnp.exp(jnp.minimum(v, 0.0)) - 1.0).astype(jnp.bfloat16)


def kernel(
    rows, cols, planes, scale,
    image, cotangent, weights,
    feat_out, grad_out, wg_out,
    wv, ft, cf, cb,
    h0, a0, h1, a1, h2, a2, ct,
    u2, r1, u1, r0, feat, grad,
    wacc, psb, prv, rsb, rsr, zr, wg,
    w_sem, in_send, in_recv, z_send, z_recv, out_send, out_recv,
    pp_send, pp_recv, rs_send, rs_recv, zz_send, zz_recv, ag_send, ag_recv, pa_send, pa_recv,
):
    gx, gy = lax.axis_index("gx"), lax.axis_index("gy")
    z, c = gx // SUB, gx % SUB
    me = gy * SUB + c
    core = c % 2
    group = rows
    width = SUB * cols
    own = pl.ds(HALO, width)
    total = width + 2 * HALO

    def at(q):
        return {"gx": z * SUB + q % SUB, "gy": q // SUB}

    def at_plane(p):
        return {"gx": p * SUB + c, "gy": gy}

    w_copy = pltpu.make_async_copy(weights, wv, w_sem)
    w_copy.start()

    barrier = pltpu.get_barrier_semaphore()

    def greet(t, carry):
        pl.semaphore_signal(barrier, inc=1, device_id=at((me + t) % group), device_id_type=pl.DeviceIdType.MESH)
        return carry

    lax.fori_loop(1, group, greet, 0)

    def greet_plane(t, carry):
        pl.semaphore_signal(barrier, inc=1, device_id=at_plane((z + t) % planes), device_id_type=pl.DeviceIdType.MESH)
        return carry

    lax.fori_loop(1, planes, greet_plane, 0)
    pl.semaphore_wait(barrier, group - 1 + planes - 1)

    def send_in(source, ext, n):
        place = ext.at[gy, pl.ds(pl.multiple_of(HALO + c * cols, 32), cols)]
        for s in range(8):
            g = lax.rem(gy + (8 - s), 8)
            for m in range(SUB):
                cc = lax.rem(c + m, SUB)
                if s == 0 and m == 0:
                    pltpu.make_async_copy(source.at[me], place, in_recv.at[n, gy]).start()
                else:
                    pltpu.make_async_remote_copy(
                        src_ref=source.at[g * SUB + cc], dst_ref=place,
                        send_sem=in_send.at[n], recv_sem=in_recv.at[n, gy],
                        device_id={"gx": z * SUB + cc, "gy": g}, device_id_type=pl.DeviceIdType.MESH,
                    ).start()

    def send_halo(ext, row, near, size, n):
        @pl.when(z < planes - 1)
        def _():
            pltpu.make_async_remote_copy(
                src_ref=ext.at[row, pl.ds(HALO + width - near - size, size)],
                dst_ref=ext.at[row, pl.ds(HALO - near - size, size)],
                send_sem=z_send.at[n, 0], recv_sem=z_recv.at[n, 0],
                device_id=at_plane(z + 1), device_id_type=pl.DeviceIdType.MESH,
            ).start()

        @pl.when(z > 0)
        def _():
            pltpu.make_async_remote_copy(
                src_ref=ext.at[row, pl.ds(HALO + near, size)],
                dst_ref=ext.at[row, pl.ds(HALO + width + near, size)],
                send_sem=z_send.at[n, 1], recv_sem=z_recv.at[n, 1],
                device_id=at_plane(z - 1), device_id_type=pl.DeviceIdType.MESH,
            ).start()

    def wait_halo(ext, near, size, n):
        @pl.when(z > 0)
        def _():
            wait_bytes(ext.at[:, pl.ds(HALO - near - size, size)], z_recv.at[n, 0])

        @pl.when(z < planes - 1)
        def _():
            wait_bytes(ext.at[:, pl.ds(HALO + width + near, size)], z_recv.at[n, 1])

    def zero_edges(ext):
        @pl.when(z == 0)
        def _():
            ext[:, 0:HALO, :] = jnp.zeros((8, HALO, 128), ext.dtype)

        @pl.when(z == planes - 1)
        def _():
            ext[:, HALO + width :, :] = jnp.zeros((8, HALO, 128), ext.dtype)

    def send_out(block, out, n):
        def one(t, carry):
            q = (me + t) % group
            pltpu.make_async_remote_copy(
                src_ref=block.at[q // SUB, pl.ds(pl.multiple_of((q % SUB) * cols, 32), cols)], dst_ref=out.at[me],
                send_sem=out_send.at[n], recv_sem=out_recv.at[n],
                device_id=at(q), device_id_type=pl.DeviceIdType.MESH,
            ).start()
            return carry

        lax.fori_loop(1, group, one, 0)
        pltpu.make_async_copy(
            block.at[gy, pl.ds(pl.multiple_of(c * cols, 32), cols)], out.at[me], out_recv.at[n]
        ).start()

    def flip(n):
        k, i, j = n // 9, n // 3 % 3, n % 3
        ft[k, i, j] = wv[k, 2 - i, 2 - j].astype(jnp.float32).T.astype(jnp.bfloat16)

    def two_rows(src, dst):
        for k in range(3):
            for j in range(3):
                base = j * 256
                dst[k, base : base + 128, 0:128] = src[k, 1, j]
                dst[k, base : base + 128, 128:256] = src[k, 0, j]
                dst[k, base + 128 : base + 256, 0:128] = src[k, 2, j]
                dst[k, base + 128 : base + 256, 128:256] = src[k, 1, j]

    send_in(image, h0, 0)
    send_in(cotangent, ct, 1)
    zero_edges(h0)
    w_copy.wait()
    two_rows(wv, cf)
    for s in range(8):
        for n in range(4 * s, min(4 * s + 4, 27)):
            flip(n)
        a = lax.rem(gy + s, 8)
        wait_bytes(h0.at[a, own], in_recv.at[0, a])
        send_halo(h0, a, 0, HALO, 0)
        a0[a, HALO : HALO + width, :] = elu(h0[a, HALO : HALO + width, :])
    for s in range(8):
        a = lax.rem(gy + s, 8)
        wait_bytes(ct.at[a, own], in_recv.at[1, a])
        send_halo(ct, a, *PIECES[0], 1)
    for n in (1, 2):
        send_halo(ct, pl.ds(0, 8), *PIECES[n], n + 1)
    zero_edges(ct)
    wait_halo(h0, 0, HALO, 0)
    for a in range(8):
        a0[a, 0:HALO, :] = elu(h0[a, 0:HALO, :])
        a0[a, HALO + width :, :] = elu(h0[a, HALO + width :, :])

    left_in = z > 0
    right_in = z < planes - 1

    def sides(near, size):
        return [(HALO - near - size, size, left_in), (HALO + width + near, size, right_in)]

    centre = [(HALO, width, None)]

    def conv(src, both, single, k, segments, merge, emit):
        step, d = STEPS[k], 32 * STEPS[k]

        def taps(rows_of, blocks):
            out = []
            for block in blocks:
                start, size, _ = block[2]
                parts = []
                for j in range(3):
                    at_col = start + (j - 1) * d
                    parts += [src[r, at_col : at_col + size, :] for r in rows_of(block)]
                out.append(jnp.concatenate(parts, axis=1))
            return out[0] if len(out) == 1 else jnp.concatenate(out, axis=0)

        def key(block):
            return block[0], block[2][0]

        def cut(value, blocks):
            pieces, at_row = {}, 0
            for block in blocks:
                size = block[2][1]
                pieces[key(block)] = value[at_row : at_row + size]
                at_row += size
            return pieces

        pairs = pairs_of(step)
        for group in [pairs] if merge else [[p] for p in pairs]:
            blocks = [(f, g, seg) for f, g in group for seg in segments]
            acc = jnp.dot(taps(lambda b: (b[0], b[1]), blocks), both[k], preferred_element_type=jnp.float32)
            first, second = cut(acc[:, 0:128], blocks), cut(acc[:, 128:256], blocks)
            above = [b for b in blocks if b[0] - step >= 0]
            below = [b for b in blocks if b[1] + step < 8]
            up, down = {}, {}
            if above:
                up = cut(
                    jnp.dot(
                        taps(lambda b: (b[0] - step,), above), single[k, 0].reshape(384, 128),
                        preferred_element_type=jnp.float32,
                    ),
                    above,
                )
            if below:
                down = cut(
                    jnp.dot(
                        taps(lambda b: (b[1] + step,), below), single[k, 2].reshape(384, 128),
                        preferred_element_type=jnp.float32,
                    ),
                    below,
                )
            for b in blocks:
                n = key(b)
                emit(b[0], *b[2], first[n] + up[n] if n in up else first[n])
                emit(b[1], *b[2], second[n] + down[n] if n in down else second[n])

    def forward(old, new, active):
        def emit(row, start, size, inside, value):
            hid = old[row, start : start + size, :].astype(jnp.float32) + value
            if inside is not None:
                hid = jnp.where(inside, hid, 0.0)
            hid = hid.astype(jnp.bfloat16)
            if active is None:
                new[row, start - HALO : start - HALO + size, :] = hid
            else:
                new[row, start : start + size, :] = hid
                active[row, start : start + size, :] = elu(hid)

        return emit

    def backward(old, hidden, new, rounded):
        def emit(row, start, size, inside, value):
            gate = jnp.exp(jnp.minimum(hidden[row, start : start + size, :].astype(jnp.float32), 0.0))
            up = old[row, start : start + size, :].astype(jnp.float32) + value * gate
            if inside is not None:
                up = jnp.where(inside, up, 0.0)
            if new is None:
                rounded[row, start - HALO : start - HALO + size, :] = up.astype(jnp.bfloat16)
            else:
                new[row, start : start + size, :] = up
                rounded[row, start : start + size, :] = up.astype(jnp.bfloat16)

        return emit

    def kernel_grad(k, active, rounded):
        step, d = STEPS[k], 32 * STEPS[k]
        runs = [(0, step, 0, 2), (step, 8 - step, 0, 3), (8 - step, 8, 1, 3)]
        wacc[...] = jnp.zeros_like(wacc)
        for q0, q1, i0, i1 in runs:
            if q1 <= q0:
                continue
            count = (q1 - q0) * width
            left = jnp.concatenate(
                [
                    active[q0:q1, HALO + (j - 1) * d : HALO + (j - 1) * d + width, :].reshape(count, 128)
                    for j in range(3)
                ],
                axis=1,
            )
            right = jnp.concatenate(
                [
                    rounded[q0 - (i - 1) * step : q1 - (i - 1) * step, HALO : HALO + width, :].reshape(count, 128)
                    for i in range(i0, i1)
                ],
                axis=1,
            )
            wacc[:, i0 * 128 : i1 * 128] += lax.dot_general(
                left, right, (((0,), (0,)), ((), ())), preferred_element_type=jnp.float32
            )
        for i in range(3):
            for j in range(3):
                psb[k, (i * 3 + j) * 128 : (i * 3 + j + 1) * 128, :] = wacc[
                    j * 128 : (j + 1) * 128, i * 128 : (i + 1) * 128
                ]
        pltpu.make_async_remote_copy(
            src_ref=psb.at[k, pl.ds(pl.multiple_of((1 - core) * HALF, 16), HALF)], dst_ref=prv.at[k],
            send_sem=pp_send.at[k], recv_sem=pp_recv.at[k],
            device_id={"gx": gx + 1 - 2 * core, "gy": gy}, device_id_type=pl.DeviceIdType.MESH,
        ).start()

    def sum_pair(k):
        wait_bytes(prv.at[k], pp_recv.at[k])
        rsb[k] = (psb[k, pl.ds(pl.multiple_of(core * HALF, 16), HALF)] + prv[k]).astype(jnp.bfloat16)
        start = lax.rem(me // 2, SLICES)
        for t in range(SLICES):
            n = lax.rem(start + t, SLICES)
            part = rsb.at[k, pl.ds(pl.multiple_of(n * SLICE, 16), SLICE)]
            place = rsr.at[k, me // 2]

            def send():
                pltpu.make_async_remote_copy(
                    src_ref=part, dst_ref=place, send_sem=rs_send.at[k], recv_sem=rs_recv.at[k],
                    device_id=at(2 * n + core), device_id_type=pl.DeviceIdType.MESH,
                ).start()

            if t > 0:
                send()
            else:
                pl.when(me >= reducers)(send)

                @pl.when(me < reducers)
                def _():
                    pltpu.make_async_copy(part, place, rs_recv.at[k]).start()

    reducers = 2 * SLICES

    def sum_plane(k):
        @pl.when(me < reducers)
        def _():
            wait_bytes(rsr.at[k], rs_recv.at[k])
            part = rsr[k, 0].astype(jnp.float32)
            for n in range(1, group // 2):
                part = part + rsr[k, n].astype(jnp.float32)
            zr[k, z] = part.astype(jnp.bfloat16)

            def one(t, carry):
                pltpu.make_async_remote_copy(
                    src_ref=zr.at[k, z], dst_ref=zr.at[k, z],
                    send_sem=zz_send.at[k], recv_sem=zz_recv.at[k],
                    device_id=at_plane((z + t) % planes), device_id_type=pl.DeviceIdType.MESH,
                ).start()
                return carry

            lax.fori_loop(1, planes, one, 0)

    def sum_planes(k):
        @pl.when(me < reducers)
        def _():
            wait_bytes(zr.at[k, pl.ds(0, planes - 1)], zz_recv.at[k])
            part = zr[k, 0].astype(jnp.float32)
            for n in range(1, planes):
                part = part + zr[k, n].astype(jnp.float32)
            place = wg.at[k, pl.ds(pl.multiple_of(core * HALF + me // 2 * SLICE, 16), SLICE)]
            place[...] = (part * scale).astype(jnp.bfloat16)
            for t in range(1, group // 2):
                pltpu.make_async_remote_copy(
                    src_ref=place, dst_ref=place, send_sem=ag_send.at[k], recv_sem=ag_recv.at[k],
                    device_id=at(lax.rem(me + 2 * t, group)), device_id_type=pl.DeviceIdType.MESH,
                ).start()

    def gather_pair(k):
        for here, count in ((me < reducers, SLICES - 1), (me >= reducers, SLICES)):
            @pl.when(here)
            def _():
                wait_bytes(wg.at[k, pl.ds(0, count * SLICE)], ag_recv.at[k])

        part = wg.at[k, pl.ds(pl.multiple_of(core * HALF, 16), HALF)]
        pltpu.make_async_remote_copy(
            src_ref=part, dst_ref=part, send_sem=pa_send.at[k], recv_sem=pa_recv.at[k],
            device_id={"gx": gx + 1 - 2 * core, "gy": gy}, device_id_type=pl.DeviceIdType.MESH,
        ).start()

    def store_grad(k):
        wait_bytes(wg.at[k, pl.ds(0, HALF)], pa_recv.at[k])
        pltpu.make_async_copy(wg.at[k], wg_out.at[k], w_sem).start()

    conv(a0, cf, wv, 0, centre, False, forward(h0, h1, a1))
    conv(a0, cf, wv, 0, sides(0, 192), False, forward(h0, h1, a1))
    conv(a1, cf, wv, 1, centre, False, forward(h1, h2, a2))
    conv(a1, cf, wv, 1, sides(0, 128), False, forward(h1, h2, a2))
    conv(a2, cf, wv, 2, centre, False, forward(h2, feat, None))
    kernel_grad(2, a2, ct)
    two_rows(ft, cb)
    sum_pair(2)
    send_out(feat, feat_out, 0)
    back2, back1 = backward(ct, h2, u2, r1), backward(u2, h1, u1, r0)
    wait_halo(ct, *PIECES[0], 1)
    conv(ct, cb, ft, 2, centre, False, back2)
    kernel_grad(1, a1, r1)
    wait_halo(ct, *PIECES[1], 2)
    conv(ct, cb, ft, 2, sides(0, 64), True, back2)
    sum_pair(1)
    conv(r1, cb, ft, 1, centre, False, back1)
    kernel_grad(0, a0, r0)
    wait_halo(ct, *PIECES[2], 3)
    conv(ct, cb, ft, 2, sides(64, 32), True, back2)
    sum_pair(0)
    conv(r1, cb, ft, 1, sides(0, 32), True, back1)
    conv(r0, cb, ft, 0, centre, False, backward(u1, h0, None, grad))
    send_out(grad, grad_out, 1)
    sum_plane(2)
    sum_plane(1)
    sum_plane(0)
    sum_planes(2)
    sum_planes(1)
    sum_planes(0)
    gather_pair(2)
    gather_pair(1)
    gather_pair(0)
    store_grad(2)
    store_grad(1)
    store_grad(0)

    wait_bytes(image.at[pl.ds(0, group - 1)], in_send.at[0])
    wait_bytes(image.at[pl.ds(0, group - 1)], in_send.at[1])
    for n, size in enumerate((HALO, 128, 64, 32)):
        @pl.when(z < planes - 1)
        def _():
            wait_bytes(h0.at[:, pl.ds(0, size)], z_send.at[n, 0])

        @pl.when(z > 0)
        def _():
            wait_bytes(h0.at[:, pl.ds(0, size)], z_send.at[n, 1])

    wait_bytes(feat_out.at[pl.ds(0, group - 1)], out_send.at[0])
    wait_bytes(feat_out, out_recv.at[0])
    for k in range(3):
        @pl.when(me < reducers)
        def _():
            wait_bytes(rsb.at[k, pl.ds(0, HALF - SLICE)], rs_send.at[k])
            wait_bytes(zr.at[k, pl.ds(0, planes - 1)], zz_send.at[k])
            wait_bytes(feat_out.at[pl.ds(0, group // 2 - 1), pl.ds(0, SLICE)], ag_send.at[k])

        @pl.when(me >= reducers)
        def _():
            wait_bytes(rsb.at[k], rs_send.at[k])

        wait_bytes(psb.at[k, pl.ds(0, HALF)], pp_send.at[k])
        wait_bytes(wg.at[k, pl.ds(0, HALF)], pa_send.at[k])
    wait_bytes(wg, w_sem)
    wait_bytes(grad_out.at[pl.ds(0, group - 1)], out_send.at[1])
    wait_bytes(grad_out, out_recv.at[1])


def finish(feat_in, grad_in, wg_in, feat_out, grad_out, wg_out, feat, grad, narrow, wide, sems):
    sources = [feat_in, grad_in] + [wg_in.at[k] for k in range(3)]
    places = [feat, grad] + [narrow.at[k] for k in range(3)]
    loads = [pltpu.make_async_copy(a, b, sems.at[n]) for n, (a, b) in enumerate(zip(sources, places))]
    sources = [feat, grad] + [wide.at[k] for k in range(3)]
    places = [feat_out, grad_out] + [wg_out.at[k] for k in range(3)]
    stores = [pltpu.make_async_copy(a, b, sems.at[5 + n]) for n, (a, b) in enumerate(zip(sources, places))]
    order = (2, 3, 4, 0, 1)
    for n in order:
        loads[n].start()
    for n in order:
        loads[n].wait()
        if n >= 2:
            wide[n - 2] = narrow[n - 2].astype(jnp.float32)
        stores[n].start()
    for copy in stores:
        copy.wait()


def solution(mesh):
    nx, ny = mesh.shape["gx"], mesh.shape["gy"]
    planes = nx // SUB

    def shards(image, cotangent, weights):
        rows, cols, ch = image.shape
        width = SUB * cols
        total = width + 2 * HALO
        scale = 1.0 / math.sqrt(rows * ny * cols * nx)
        bf, f32 = jnp.bfloat16, jnp.float32
        dma = pltpu.SemaphoreType.DMA
        ext = pltpu.VMEM((ny, total, ch), bf)
        ext32 = pltpu.VMEM((ny, total, ch), f32)
        body = functools.partial(kernel, rows, cols, planes, scale)
        features, grad, wg = pl.pallas_call(
            body,
            out_shape=(
                jax.ShapeDtypeStruct(image.shape, bf),
                jax.ShapeDtypeStruct(image.shape, bf),
                jax.ShapeDtypeStruct((3, 9 * ch, ch), bf),
            ),
            in_specs=[pl.BlockSpec(memory_space=pl.ANY)] * 3,
            out_specs=[pl.BlockSpec(memory_space=pl.ANY)] * 3,
            scratch_shapes=[
                pltpu.VMEM((3, 3, 3, ch, ch), bf),
                pltpu.VMEM((3, 3, 3, ch, ch), bf),
                pltpu.VMEM((3, 6 * ch, 2 * ch), bf),
                pltpu.VMEM((3, 6 * ch, 2 * ch), bf),
                ext, ext, ext, ext, ext, ext, ext,
                ext32, ext, ext32, ext,
                pltpu.VMEM((ny, width, ch), bf),
                pltpu.VMEM((ny, width, ch), bf),
                pltpu.VMEM((3 * ch, 3 * ch), f32),
                pltpu.VMEM((3, 2 * HALF, ch), f32),
                pltpu.VMEM((3, HALF, ch), f32),
                pltpu.VMEM((3, HALF, ch), bf),
                pltpu.VMEM((3, rows // 2, SLICE, ch), bf),
                pltpu.VMEM((3, planes, SLICE, ch), bf),
                pltpu.VMEM((3, 2 * HALF, ch), bf),
                dma,
                dma((2,)), dma((2, ny)), dma((4, 2)), dma((4, 2)), dma((2,)), dma((2,)),
                *[dma((3,))] * 10,
            ],
            compiler_params=pltpu.CompilerParams(
                collective_id=0, has_side_effects=True, vmem_limit_bytes=56 * 1024 * 1024
            ),
        )(image, cotangent, weights)
        features, grad, wg = pl.pallas_call(
            finish,
            out_shape=(
                jax.ShapeDtypeStruct(image.shape, bf),
                jax.ShapeDtypeStruct(image.shape, bf),
                jax.ShapeDtypeStruct((3, 9 * ch, ch), f32),
            ),
            in_specs=[pl.BlockSpec(memory_space=pl.ANY)] * 3,
            out_specs=[pl.BlockSpec(memory_space=pl.ANY)] * 3,
            scratch_shapes=[
                pltpu.VMEM(image.shape, bf),
                pltpu.VMEM(image.shape, bf),
                pltpu.VMEM((3, 9 * ch, ch), bf),
                pltpu.VMEM((3, 9 * ch, ch), f32),
                dma((10,)),
            ],
            compiler_params=pltpu.CompilerParams(vmem_limit_bytes=56 * 1024 * 1024),
        )(features, grad, wg)
        return features, grad, wg.reshape(3, 3, 3, ch, ch)

    return jax.shard_map(
        shards,
        mesh=mesh,
        in_specs=(P("gy", "gx", None), P("gy", "gx", None), P()),
        out_specs=(P("gy", "gx", None), P("gy", "gx", None), P()),
        check_vma=False,
    )
```

```python
import functools
import math

import jax
import jax.numpy as jnp
from jax import lax
from jax.experimental import pallas as pl
from jax.experimental.pallas import tpu as pltpu
from jax.sharding import PartitionSpec as P

SUB = 4
HALO = 224
STEPS = (1, 2, 4)
PIECES = ((0, 128), (128, 64), (192, 32))
SLICE, SLICES = 48, 12
HALF = SLICE * SLICES


def pairs_of(step):
    return [(o, o + step) for o in range(8) if (o // step) % 2 == 0]


def wait_bytes(ref, sem):
    pltpu.make_async_copy(ref, ref, sem).wait()


def elu(h):
    v = h.astype(jnp.float32)
    return jnp.where(v > 0, v, jnp.exp(jnp.minimum(v, 0.0)) - 1.0).astype(jnp.bfloat16)


def kernel(
    rows, cols, planes, scale,
    image, cotangent, weights,
    feat_out, grad_out, wg_out,
    wv, ft, cf, cb,
    h0, a0, h1, a1, h2, a2, ct,
    u2, r1, u1, r0, feat, grad,
    wacc, psb, prv, rsb, rsr, zr, wg,
    w_sem, in_send, in_recv, z_send, z_recv, out_send, out_recv,
    pp_send, pp_recv, rs_send, rs_recv, zz_send, zz_recv, ag_send, ag_recv, pa_send, pa_recv,
):
    gx, gy = lax.axis_index("gx"), lax.axis_index("gy")
    z, c = lax.div(gx, SUB), lax.rem(gx, SUB)
    me = gy * SUB + c
    core, y_lo = lax.rem(c, 2), lax.div(c, 2)
    pair = gy * 2 + y_lo
    group = rows
    width = SUB * cols
    own = pl.ds(HALO, width)
    total = width + 2 * HALO

    def at_plane(p):
        return {"gx": p * SUB + c, "gy": gy}

    w_copy = pltpu.make_async_copy(weights, wv, w_sem)
    w_copy.start()

    barrier = pltpu.get_barrier_semaphore()

    for p in range(1, planes):
        pl.semaphore_signal(
            barrier, inc=1, device_id=at_plane(lax.rem(z + p, planes)), device_id_type=pl.DeviceIdType.MESH
        )
    for s in reversed(range(8)):
        g = lax.rem(gy + s, 8)
        for m in range(SUB):
            if s or m:
                pl.semaphore_signal(
                    barrier, inc=1, device_id={"gx": z * SUB + lax.rem(c + m, SUB), "gy": g},
                    device_id_type=pl.DeviceIdType.MESH,
                )
    pl.semaphore_wait(barrier, group - 1 + planes - 1)

    def send_in(source, ext, n):
        place = ext.at[gy, pl.ds(pl.multiple_of(HALO + c * cols, 32), cols)]
        for s in range(8):
            g = lax.rem(gy + (8 - s), 8)
            for m in range(SUB):
                cc = lax.rem(c + m, SUB)
                if s == 0 and m == 0:
                    pltpu.make_async_copy(source.at[me], place, in_recv.at[n, gy]).start()
                else:
                    pltpu.make_async_remote_copy(
                        src_ref=source.at[g * SUB + cc], dst_ref=place,
                        send_sem=in_send.at[n], recv_sem=in_recv.at[n, gy],
                        device_id={"gx": z * SUB + cc, "gy": g}, device_id_type=pl.DeviceIdType.MESH,
                    ).start()

    def send_halo(ext, row, near, size, n):
        @pl.when(z < planes - 1)
        def _():
            pltpu.make_async_remote_copy(
                src_ref=ext.at[row, pl.ds(HALO + width - near - size, size)],
                dst_ref=ext.at[row, pl.ds(HALO - near - size, size)],
                send_sem=z_send.at[n, 0], recv_sem=z_recv.at[n, 0],
                device_id=at_plane(z + 1), device_id_type=pl.DeviceIdType.MESH,
            ).start()

        @pl.when(z > 0)
        def _():
            pltpu.make_async_remote_copy(
                src_ref=ext.at[row, pl.ds(HALO + near, size)],
                dst_ref=ext.at[row, pl.ds(HALO + width + near, size)],
                send_sem=z_send.at[n, 1], recv_sem=z_recv.at[n, 1],
                device_id=at_plane(z - 1), device_id_type=pl.DeviceIdType.MESH,
            ).start()

    def wait_halo(ext, near, size, n):
        @pl.when(z > 0)
        def _():
            wait_bytes(ext.at[:, pl.ds(HALO - near - size, size)], z_recv.at[n, 0])

        @pl.when(z < planes - 1)
        def _():
            wait_bytes(ext.at[:, pl.ds(HALO + width + near, size)], z_recv.at[n, 1])

    def zero_edges(ext):
        @pl.when(z == 0)
        def _():
            ext[:, 0:HALO, :] = jnp.zeros((8, HALO, 128), ext.dtype)

        @pl.when(z == planes - 1)
        def _():
            ext[:, HALO + width :, :] = jnp.zeros((8, HALO, 128), ext.dtype)

    def send_out(block, out, n):
        place = out.at[me]
        for s in range(8):
            g = lax.rem(gy + s, 8)
            for m in range(SUB):
                cc = lax.rem(c + m, SUB)
                part = block.at[g, pl.ds(pl.multiple_of(cc * cols, 32), cols)]
                if s == 0 and m == 0:
                    pltpu.make_async_copy(part, place, out_recv.at[n]).start()
                else:
                    pltpu.make_async_remote_copy(
                        src_ref=part, dst_ref=place, send_sem=out_send.at[n], recv_sem=out_recv.at[n],
                        device_id={"gx": z * SUB + cc, "gy": g}, device_id_type=pl.DeviceIdType.MESH,
                    ).start()

    def flip(n):
        k, i, j = n // 9, n // 3 % 3, n % 3
        ft[k, i, j] = wv[k, 2 - i, 2 - j].astype(jnp.float32).T.astype(jnp.bfloat16)

    def two_rows(src, dst):
        for k in range(3):
            for j in range(3):
                base = j * 256
                dst[k, base : base + 128, 0:128] = src[k, 1, j]
                dst[k, base : base + 128, 128:256] = src[k, 0, j]
                dst[k, base + 128 : base + 256, 0:128] = src[k, 2, j]
                dst[k, base + 128 : base + 256, 128:256] = src[k, 1, j]

    send_in(image, h0, 0)
    send_in(cotangent, ct, 1)
    zero_edges(h0)
    w_copy.wait()
    two_rows(wv, cf)
    for s in range(8):
        for n in range(4 * s, min(4 * s + 4, 27)):
            flip(n)
        a = lax.rem(gy + s, 8)
        wait_bytes(h0.at[a, own], in_recv.at[0, a])
        send_halo(h0, a, 0, HALO, 0)
        a0[a, HALO : HALO + width, :] = elu(h0[a, HALO : HALO + width, :])
    for s in range(8):
        a = lax.rem(gy + s, 8)
        wait_bytes(ct.at[a, own], in_recv.at[1, a])
        send_halo(ct, a, *PIECES[0], 1)
    for n in (1, 2):
        send_halo(ct, pl.ds(0, 8), *PIECES[n], n + 1)
    zero_edges(ct)
    wait_halo(h0, 0, HALO, 0)
    for a in range(8):
        a0[a, 0:HALO, :] = elu(h0[a, 0:HALO, :])
        a0[a, HALO + width :, :] = elu(h0[a, HALO + width :, :])

    left_in = z > 0
    right_in = z < planes - 1

    def sides(near, size):
        return [(HALO - near - size, size, left_in), (HALO + width + near, size, right_in)]

    centre = [(HALO, width, None)]

    def conv(src, both, single, k, segments, merge, emit):
        step, d = STEPS[k], 32 * STEPS[k]

        def taps(rows_of, blocks):
            out = []
            for block in blocks:
                start, size, _ = block[2]
                parts = []
                for j in range(3):
                    at_col = start + (j - 1) * d
                    parts += [src[r, at_col : at_col + size, :] for r in rows_of(block)]
                out.append(jnp.concatenate(parts, axis=1))
            return out[0] if len(out) == 1 else jnp.concatenate(out, axis=0)

        def key(block):
            return block[0], block[2][0]

        def cut(value, blocks):
            pieces, at_row = {}, 0
            for block in blocks:
                size = block[2][1]
                pieces[key(block)] = value[at_row : at_row + size]
                at_row += size
            return pieces

        pairs = pairs_of(step)
        for group in [pairs] if merge else [[p] for p in pairs]:
            blocks = [(f, g, seg) for f, g in group for seg in segments]
            acc = jnp.dot(taps(lambda b: (b[0], b[1]), blocks), both[k], preferred_element_type=jnp.float32)
            first, second = cut(acc[:, 0:128], blocks), cut(acc[:, 128:256], blocks)
            above = [b for b in blocks if b[0] - step >= 0]
            below = [b for b in blocks if b[1] + step < 8]
            up, down = {}, {}
            if above:
                up = cut(
                    jnp.dot(
                        taps(lambda b: (b[0] - step,), above), single[k, 0].reshape(384, 128),
                        preferred_element_type=jnp.float32,
                    ),
                    above,
                )
            if below:
                down = cut(
                    jnp.dot(
                        taps(lambda b: (b[1] + step,), below), single[k, 2].reshape(384, 128),
                        preferred_element_type=jnp.float32,
                    ),
                    below,
                )
            for b in blocks:
                n = key(b)
                emit(b[0], *b[2], first[n] + up[n] if n in up else first[n])
                emit(b[1], *b[2], second[n] + down[n] if n in down else second[n])

    def forward(old, new, active):
        def emit(row, start, size, inside, value):
            hid = old[row, start : start + size, :].astype(jnp.float32) + value
            if inside is not None:
                hid = jnp.where(inside, hid, 0.0)
            hid = hid.astype(jnp.bfloat16)
            if active is None:
                new[row, start - HALO : start - HALO + size, :] = hid
            else:
                new[row, start : start + size, :] = hid
                active[row, start : start + size, :] = elu(hid)

        return emit

    def backward(old, hidden, new, rounded):
        def emit(row, start, size, inside, value):
            gate = jnp.exp(jnp.minimum(hidden[row, start : start + size, :].astype(jnp.float32), 0.0))
            up = old[row, start : start + size, :].astype(jnp.float32) + value * gate
            if inside is not None:
                up = jnp.where(inside, up, 0.0)
            if new is None:
                rounded[row, start - HALO : start - HALO + size, :] = up.astype(jnp.bfloat16)
            else:
                new[row, start : start + size, :] = up
                rounded[row, start : start + size, :] = up.astype(jnp.bfloat16)

        return emit

    def kernel_grad(k, active, rounded):
        step, d = STEPS[k], 32 * STEPS[k]
        runs = [(0, step, 0, 2), (step, 8 - step, 0, 3), (8 - step, 8, 1, 3)]
        wacc[...] = jnp.zeros_like(wacc)
        for q0, q1, i0, i1 in runs:
            if q1 <= q0:
                continue
            count = (q1 - q0) * width
            left = jnp.concatenate(
                [
                    active[q0:q1, HALO + (j - 1) * d : HALO + (j - 1) * d + width, :].reshape(count, 128)
                    for j in range(3)
                ],
                axis=1,
            )
            right = jnp.concatenate(
                [
                    rounded[q0 - (i - 1) * step : q1 - (i - 1) * step, HALO : HALO + width, :].reshape(count, 128)
                    for i in range(i0, i1)
                ],
                axis=1,
            )
            wacc[:, i0 * 128 : i1 * 128] += lax.dot_general(
                left, right, (((0,), (0,)), ((), ())), preferred_element_type=jnp.float32
            )
        for i in range(3):
            for j in range(3):
                psb[k, (i * 3 + j) * 128 : (i * 3 + j + 1) * 128, :] = wacc[
                    j * 128 : (j + 1) * 128, i * 128 : (i + 1) * 128
                ]
        pltpu.make_async_remote_copy(
            src_ref=psb.at[k, pl.ds(pl.multiple_of((1 - core) * HALF, 16), HALF)], dst_ref=prv.at[k],
            send_sem=pp_send.at[k], recv_sem=pp_recv.at[k],
            device_id={"gx": gx + 1 - 2 * core, "gy": gy}, device_id_type=pl.DeviceIdType.MESH,
        ).start()

    def sum_pair(k):
        wait_bytes(prv.at[k], pp_recv.at[k])
        rsb[k] = (psb[k, pl.ds(pl.multiple_of(core * HALF, 16), HALF)] + prv[k]).astype(jnp.bfloat16)
        start = lax.rem(pair, SLICES)
        for t in range(SLICES):
            n = lax.rem(start + t, SLICES)
            part = rsb.at[k, pl.ds(pl.multiple_of(n * SLICE, 16), SLICE)]
            place = rsr.at[k, pair]

            def send():
                pltpu.make_async_remote_copy(
                    src_ref=part, dst_ref=place, send_sem=rs_send.at[k], recv_sem=rs_recv.at[k],
                    device_id={"gx": z * SUB + lax.rem(n, 2) * 2 + core, "gy": lax.div(n, 2)},
                    device_id_type=pl.DeviceIdType.MESH,
                ).start()

            if t > 0:
                send()
            else:
                pl.when(me >= reducers)(send)

                @pl.when(me < reducers)
                def _():
                    pltpu.make_async_copy(part, place, rs_recv.at[k]).start()

    reducers = 2 * SLICES

    def sum_plane(k):
        @pl.when(me < reducers)
        def _():
            wait_bytes(rsr.at[k], rs_recv.at[k])
            part = rsr[k, 0].astype(jnp.float32)
            for n in range(1, group // 2):
                part = part + rsr[k, n].astype(jnp.float32)
            zr[k, z] = part.astype(jnp.bfloat16)

            for p in range(1, planes):
                pltpu.make_async_remote_copy(
                    src_ref=zr.at[k, z], dst_ref=zr.at[k, z],
                    send_sem=zz_send.at[k], recv_sem=zz_recv.at[k],
                    device_id=at_plane(lax.rem(z + p, planes)), device_id_type=pl.DeviceIdType.MESH,
                ).start()

    def sum_planes(k):
        @pl.when(me < reducers)
        def _():
            wait_bytes(zr.at[k, pl.ds(0, planes - 1)], zz_recv.at[k])
            part = zr[k, 0].astype(jnp.float32)
            for n in range(1, planes):
                part = part + zr[k, n].astype(jnp.float32)
            place = wg.at[k, pl.ds(pl.multiple_of(core * HALF + pair * SLICE, 16), SLICE)]
            place[...] = (part * scale).astype(jnp.bfloat16)
            for s in range(8):
                g = lax.rem(gy + s, 8)
                for m in range(2):
                    if s or m:
                        pltpu.make_async_remote_copy(
                            src_ref=place, dst_ref=place, send_sem=ag_send.at[k], recv_sem=ag_recv.at[k],
                            device_id={"gx": z * SUB + lax.rem(y_lo + m, 2) * 2 + core, "gy": g},
                            device_id_type=pl.DeviceIdType.MESH,
                        ).start()

    def gather_pair(k):
        for here, count in ((me < reducers, SLICES - 1), (me >= reducers, SLICES)):
            @pl.when(here)
            def _():
                wait_bytes(wg.at[k, pl.ds(0, count * SLICE)], ag_recv.at[k])

        part = wg.at[k, pl.ds(pl.multiple_of(core * HALF, 16), HALF)]
        pltpu.make_async_remote_copy(
            src_ref=part, dst_ref=part, send_sem=pa_send.at[k], recv_sem=pa_recv.at[k],
            device_id={"gx": gx + 1 - 2 * core, "gy": gy}, device_id_type=pl.DeviceIdType.MESH,
        ).start()

    def store_grad(k):
        wait_bytes(wg.at[k, pl.ds(0, HALF)], pa_recv.at[k])
        pltpu.make_async_copy(wg.at[k], wg_out.at[k], w_sem).start()

    conv(a0, cf, wv, 0, centre, False, forward(h0, h1, a1))
    conv(a0, cf, wv, 0, sides(0, 192), False, forward(h0, h1, a1))
    conv(a1, cf, wv, 1, centre, False, forward(h1, h2, a2))
    conv(a1, cf, wv, 1, sides(0, 128), False, forward(h1, h2, a2))
    conv(a2, cf, wv, 2, centre, False, forward(h2, feat, None))
    kernel_grad(2, a2, ct)
    two_rows(ft, cb)
    sum_pair(2)
    back2, back1 = backward(ct, h2, u2, r1), backward(u2, h1, u1, r0)
    wait_halo(ct, *PIECES[0], 1)
    conv(ct, cb, ft, 2, centre, False, back2)
    kernel_grad(1, a1, r1)
    wait_halo(ct, *PIECES[1], 2)
    conv(ct, cb, ft, 2, sides(0, 64), True, back2)
    sum_pair(1)
    conv(r1, cb, ft, 1, centre, False, back1)
    kernel_grad(0, a0, r0)
    wait_halo(ct, *PIECES[2], 3)
    conv(ct, cb, ft, 2, sides(64, 32), True, back2)
    sum_pair(0)
    send_out(feat, feat_out, 0)
    conv(r1, cb, ft, 1, sides(0, 32), True, back1)
    conv(r0, cb, ft, 0, centre, False, backward(u1, h0, None, grad))
    send_out(grad, grad_out, 1)
    sum_plane(2)
    sum_plane(1)
    sum_plane(0)
    sum_planes(2)
    sum_planes(1)
    sum_planes(0)
    gather_pair(2)
    gather_pair(1)
    gather_pair(0)
    store_grad(2)
    store_grad(1)
    store_grad(0)

    wait_bytes(image.at[pl.ds(0, group - 1)], in_send.at[0])
    wait_bytes(image.at[pl.ds(0, group - 1)], in_send.at[1])
    for n, size in enumerate((HALO, 128, 64, 32)):
        @pl.when(z < planes - 1)
        def _():
            wait_bytes(h0.at[:, pl.ds(0, size)], z_send.at[n, 0])

        @pl.when(z > 0)
        def _():
            wait_bytes(h0.at[:, pl.ds(0, size)], z_send.at[n, 1])

    wait_bytes(feat_out.at[pl.ds(0, group - 1)], out_send.at[0])
    wait_bytes(feat_out, out_recv.at[0])
    for k in range(3):
        @pl.when(me < reducers)
        def _():
            wait_bytes(rsb.at[k, pl.ds(0, HALF - SLICE)], rs_send.at[k])
            wait_bytes(zr.at[k, pl.ds(0, planes - 1)], zz_send.at[k])
            wait_bytes(feat_out.at[pl.ds(0, group // 2 - 1), pl.ds(0, SLICE)], ag_send.at[k])

        @pl.when(me >= reducers)
        def _():
            wait_bytes(rsb.at[k], rs_send.at[k])

        wait_bytes(psb.at[k, pl.ds(0, HALF)], pp_send.at[k])
        wait_bytes(wg.at[k, pl.ds(0, HALF)], pa_send.at[k])
    wait_bytes(wg, w_sem)
    wait_bytes(grad_out.at[pl.ds(0, group - 1)], out_send.at[1])
    wait_bytes(grad_out, out_recv.at[1])


def finish(feat_in, grad_in, wg_in, feat_out, grad_out, wg_out, feat, grad, narrow, wide, sems):
    sources = [feat_in, grad_in] + [wg_in.at[k] for k in range(3)]
    places = [feat, grad] + [narrow.at[k] for k in range(3)]
    loads = [pltpu.make_async_copy(a, b, sems.at[n]) for n, (a, b) in enumerate(zip(sources, places))]
    sources = [feat, grad] + [wide.at[k] for k in range(3)]
    places = [feat_out, grad_out] + [wg_out.at[k] for k in range(3)]
    stores = [pltpu.make_async_copy(a, b, sems.at[5 + n]) for n, (a, b) in enumerate(zip(sources, places))]
    order = (2, 3, 4, 0, 1)
    for n in order:
        loads[n].start()
    for n in order:
        loads[n].wait()
        if n >= 2:
            wide[n - 2] = narrow[n - 2].astype(jnp.float32)
        stores[n].start()
    for copy in stores:
        copy.wait()


def solution(mesh):
    nx, ny = mesh.shape["gx"], mesh.shape["gy"]
    planes = nx // SUB

    def shards(image, cotangent, weights):
        rows, cols, ch = image.shape
        width = SUB * cols
        total = width + 2 * HALO
        scale = 1.0 / math.sqrt(rows * ny * cols * nx)
        bf, f32 = jnp.bfloat16, jnp.float32
        dma = pltpu.SemaphoreType.DMA
        ext = pltpu.VMEM((ny, total, ch), bf)
        ext32 = pltpu.VMEM((ny, total, ch), f32)
        body = functools.partial(kernel, rows, cols, planes, scale)
        features, grad, wg = pl.pallas_call(
            body,
            out_shape=(
                jax.ShapeDtypeStruct(image.shape, bf),
                jax.ShapeDtypeStruct(image.shape, bf),
                jax.ShapeDtypeStruct((3, 9 * ch, ch), bf),
            ),
            in_specs=[pl.BlockSpec(memory_space=pl.ANY)] * 3,
            out_specs=[pl.BlockSpec(memory_space=pl.ANY)] * 3,
            scratch_shapes=[
                pltpu.VMEM((3, 3, 3, ch, ch), bf),
                pltpu.VMEM((3, 3, 3, ch, ch), bf),
                pltpu.VMEM((3, 6 * ch, 2 * ch), bf),
                pltpu.VMEM((3, 6 * ch, 2 * ch), bf),
                ext, ext, ext, ext, ext, ext, ext,
                ext32, ext, ext32, ext,
                pltpu.VMEM((ny, width, ch), bf),
                pltpu.VMEM((ny, width, ch), bf),
                pltpu.VMEM((3 * ch, 3 * ch), f32),
                pltpu.VMEM((3, 2 * HALF, ch), f32),
                pltpu.VMEM((3, HALF, ch), f32),
                pltpu.VMEM((3, HALF, ch), bf),
                pltpu.VMEM((3, rows // 2, SLICE, ch), bf),
                pltpu.VMEM((3, planes, SLICE, ch), bf),
                pltpu.VMEM((3, 2 * HALF, ch), bf),
                dma,
                dma((2,)), dma((2, ny)), dma((4, 2)), dma((4, 2)), dma((2,)), dma((2,)),
                *[dma((3,))] * 10,
            ],
            compiler_params=pltpu.CompilerParams(
                collective_id=0, has_side_effects=True, vmem_limit_bytes=56 * 1024 * 1024
            ),
        )(image, cotangent, weights)
        features, grad, wg = pl.pallas_call(
            finish,
            out_shape=(
                jax.ShapeDtypeStruct(image.shape, bf),
                jax.ShapeDtypeStruct(image.shape, bf),
                jax.ShapeDtypeStruct((3, 9 * ch, ch), f32),
            ),
            in_specs=[pl.BlockSpec(memory_space=pl.ANY)] * 3,
            out_specs=[pl.BlockSpec(memory_space=pl.ANY)] * 3,
            scratch_shapes=[
                pltpu.VMEM(image.shape, bf),
                pltpu.VMEM(image.shape, bf),
                pltpu.VMEM((3, 9 * ch, ch), bf),
                pltpu.VMEM((3, 9 * ch, ch), f32),
                dma((10,)),
            ],
            compiler_params=pltpu.CompilerParams(vmem_limit_bytes=56 * 1024 * 1024),
        )(features, grad, wg)
        return features, grad, wg.reshape(3, 3, 3, ch, ch)

    return jax.shard_map(
        shards,
        mesh=mesh,
        in_specs=(P("gy", "gx", None), P("gy", "gx", None), P()),
        out_specs=(P("gy", "gx", None), P("gy", "gx", None), P()),
        check_vma=False,
    )
```
